256 devices in a mesh: cand: 32 (over y, z_hi, x), tp: 8 (over z_lo, core).
Axes of the slice: x: 4, y: 4, z: 8 (z_hi: 2, z_lo: 4; z = z_hi * 4 + z_lo), core: 2. Of those that a mesh axis runs over, the one named last changes fastest.
Arguments:
- layer_input: bfloat16 [32, 256, 8192], P('cand', None, 'tp'), may hold values from -1200 to 1200
- coef_index: int32 [32, 4, 3], replicated, may hold values from 0 to 24
- lengths: int32 [32, 8], P('cand'), may hold values from 1 to 64, 256 in all within a row
- src_gain: bfloat16 [3, 8192], replicated, may hold values from 0.099609375 to 1.8984375
- src_query: bfloat16 [3, 8192, 4096], P(None, ('tp', 'cand')), may hold values from -0.0625 to 0.0625
- src_key: bfloat16 [3, 8192, 1024], P(None, ('tp', 'cand')), may hold values from -0.0625 to 0.0625
- src_value: bfloat16 [3, 8192, 1024], P(None, ('tp', 'cand')), may hold values from -0.0625 to 0.0625
- src_qbias: bfloat16 [3, 4096], replicated, may hold values from -3 to 3
- src_kbias: bfloat16 [3, 1024], replicated, may hold values from -64 to 64
- src_vbias: bfloat16 [3, 1024], replicated, may hold values from -3 to 3
Outputs:
- attention_out: bfloat16 [32, 256, 4096], P('cand', None, 'tp')
The draws below stay inside these ranges and needn't reach their ends.
Inputs may be any that keep to these rules, and one draw needn't show every extreme that they name: Each candidate's 8 lengths add up to 256.
All inputs are finite; a program needn't handle non-finite values.
Results may differ from the reference program's by a relative error of at most 0.012.
The reference program's roundings to bfloat16 on the way (of `query_weight`, `normed`, `values` and `shares`) count: a program that leaves them out, or rounds other values in their place, can miss the bound.
Values may be sent and summed in bfloat16 or wider, within the bound.
No kernel may reach another device: no remote copies, remote signals or barrier semaphores. Data moves between devices by JAX's collectives and lax.ppermute only.
A program may use at most 128 MiB of HBM per device.

```python
import math
import jax
import jax.numpy as jnp
import numpy as np
from jax import lax

D = 8192
QH = 32
KVH = 8
DH = 128
TOK = 256
NDOC = 8
DOC_MOST = 64
CANDS = 32
QW = 4096
KW = 1024


def draw_layer_input(key, part):
    key = jax.random.fold_in(key, 11)
    keys = jax.random.split(key, 3)
    shape = (CANDS, TOK, D)
    row_scale = jnp.exp(jax.random.uniform(keys[0], (CANDS, TOK, 1), minval=0.0, maxval=2.3))
    ramp = 1.0 + 2.0 * jnp.arange(D).astype(jnp.float32) / D
    column_scale = jnp.exp(jax.random.uniform(keys[1], (1, 1, D), minval=0.0, maxval=2.3)) * ramp
    base = jax.random.truncated_normal(keys[2], -4.0, 4.0, shape)
    return (base * row_scale * column_scale).astype(jnp.bfloat16)


def draw_src_kbias(key, part):
    key = jax.random.fold_in(key, 23)
    shape = (3, KVH * DH)
    values = jax.random.truncated_normal(key, -4.0, 4.0, shape)
    return values.astype(jnp.bfloat16)


def place_ends(values, stream_key, low, largest):
    longest = values.shape.index(max(values.shape))
    spots = []
    for shift in (0, 1):
        where = [jax.random.randint(jax.random.fold_in(stream_key, axis), (), 0, length) for axis, length in enumerate(values.shape)]
        where[longest] = (where[longest] + shift) % values.shape[longest]
        spots.append(tuple(where))
    return values.at[spots[0]].set(low).at[spots[1]].set(largest)


def block_levels(key, dims, pieces, smallest, high):
    def one(axis_at, blocks):
        heights = jax.random.uniform(jax.random.fold_in(jax.random.fold_in(key, 6), axis_at), (blocks,), jnp.float32, smallest / len(pieces), high / len(pieces))
        return jnp.repeat(jnp.exp(heights), dims[axis_at] // blocks).reshape((-1,) + (1,) * (len(dims) - axis_at - 1))

    level = one(*pieces[0])
    for cut in pieces[1:]:
        level = level * one(*cut)
    return level


def split_up(number_of, total, limit, lean):
    weights = [(1 << 20) // math.isqrt(standing ** lean) + 1 for standing in range(2, number_of + 1)]
    surplus, given = total - limit - (number_of - 1), [1] * (number_of - 1)
    while surplus > 0:
        movable = [i for i in range(number_of - 1) if given[i] < limit]
        mass, left = sum([weights[i] for i in movable]), surplus
        for i in movable:
            addition = min(limit - given[i], max(1, left * weights[i] // mass), surplus)
            given[i] = given[i] + addition
            surplus = surplus - addition
    return np.array([limit] + given)


def uneven(stream_key, count, total, most, skew):
    if count == 2:
        one = jax.random.randint(stream_key, (), max(1, total - most), min(most, total - 1) + 1)
        return jnp.stack([one, total - one])
    sizes = jnp.asarray(split_up(count, total, most, skew), jnp.int32)
    pairs = (count - 1) // 2
    giver, receiver = sizes[1:1 + 2 * pairs:2], sizes[2:2 + 2 * pairs:2]
    slack = jnp.minimum(giver - 1, most - receiver)
    passed = jax.random.randint(jax.random.fold_in(stream_key, 1), (pairs,), 0, 1 << 20) % (slack + 1)
    sizes = sizes.at[1:1 + 2 * pairs:2].set(giver - passed).at[2:2 + 2 * pairs:2].set(receiver + passed)
    return sizes[jax.random.permutation(jax.random.fold_in(stream_key, 2), count)]


def noise(key, extent, scale, bound, pieces=(), dtype=jnp.bfloat16):
    factor_of = block_levels(key, extent, pieces, -0.22, 0.18) if pieces else 1.0
    array = jax.random.normal(key, extent, jnp.float32) * scale * factor_of
    return jnp.minimum(jnp.maximum(array, -bound), bound).astype(dtype)


def setup_inputs(seed: int = 0) -> dict:
    key_of = jax.random.split(jax.random.key(seed), 11)
    layer_input = draw_layer_input(jax.random.fold_in(key_of[10], 71), 0)
    coef_index = place_ends(jax.random.randint(key_of[1], (CANDS, 4, 3), 0, 25), jax.random.fold_in(key_of[1], 1), 0, 24).astype(jnp.int32)
    lengths = jax.vmap(lambda own: uneven(own, NDOC, TOK, DOC_MOST, 1))(jax.random.split(key_of[2], CANDS)).reshape((CANDS, NDOC)).astype(jnp.int32)
    src_gain = jnp.clip(1.0 + 0.18 * jax.random.normal(key_of[3], (3, D), jnp.float32), 0.099609375, 1.8984375).astype(jnp.bfloat16)
    src_query = noise(key_of[4], (3, D, QW), D ** -0.5, 0.0625, ((1, 256),))
    src_key = noise(key_of[5], (3, D, KW), D ** -0.5, 0.0625, ((1, 256),))
    src_value = noise(key_of[6], (3, D, KW), D ** -0.5, 0.0625, ((1, 256),))
    src_qbias = noise(key_of[7], (3, QW), 0.5, 3.0)
    src_kbias = draw_src_kbias(jax.random.fold_in(key_of[10], 71), 0)
    src_vbias = noise(key_of[9], (3, KW), 0.5, 3.0)
    return dict(layer_input=layer_input, coef_index=coef_index, lengths=lengths, src_gain=src_gain, src_query=src_query, src_key=src_key, src_value=src_value, src_qbias=src_qbias, src_kbias=src_kbias, src_vbias=src_vbias)


eps_norm = 1e-06
rope_base = 1000000.0

def coefficients(coef_index):
    return (coef_index.astype(jnp.float32) - 4.0) / 16.0

def blend_small(mixing, source):
    return mixing[0] * source[0].astype(jnp.float32) + mixing[1] * source[1].astype(jnp.float32) + mixing[2] * source[2].astype(jnp.float32)

def rope_tables(row_count, head_size):
    positions = jnp.arange(row_count).astype(jnp.float32)
    exponent = jnp.arange(0, head_size, 2).astype(jnp.float32) / head_size
    inverse = rope_base ** (-exponent)
    angle_table = positions[:, None] * inverse[None, :]
    return (jnp.cos(angle_table), jnp.sin(angle_table))

def rotate(matrix, cosine_table, sine_table):
    middle = matrix.shape[-1] // 2
    leading = matrix[..., :middle]
    trailing = matrix[..., middle:]
    return jnp.concatenate([leading * cosine_table - trailing * sine_table, trailing * cosine_table + leading * sine_table], axis=-1)

def document_mask(length_row, row_count):
    doc_ends = jnp.cumsum(length_row.astype(jnp.int32))
    positions = jnp.arange(row_count).astype(jnp.int32)
    owners = lax.optimization_barrier(jnp.sum((positions[:, None] >= doc_ends[None, :]).astype(jnp.int32), axis=1))
    return (owners[:, None] == owners[None, :]) & (positions[:, None] >= positions[None, :])

def attention_shares(queries, key_rows, allowed):
    scores = jnp.einsum('tgqd,sgd->gqts', queries, key_rows, precision=lax.Precision.HIGHEST)
    scores = scores * queries.shape[-1] ** (-0.5)
    scores = jnp.where(allowed[None, None], scores, -1e+30)
    highest = lax.optimization_barrier(jnp.max(scores, axis=-1, keepdims=True))
    powers = jnp.exp(scores - highest)
    return (powers / lax.optimization_barrier(jnp.sum(powers, axis=-1, keepdims=True))).astype(jnp.bfloat16)

def reference(layer_input, coef_index, lengths, src_gain, src_query, src_key, src_value, src_qbias, src_kbias, src_vbias):
    cosine_table, sine_table = rope_tables(TOK, DH)
    per_group = QH // KVH

    def candidate(packed):
        inputs, index_row, length_row = packed
        mixing = coefficients(index_row)
        gain_row = blend_small(mixing[0], src_gain)
        features = inputs.astype(jnp.float32)
        scale = lax.rsqrt(lax.optimization_barrier(jnp.mean(features * features, axis=-1, keepdims=True)) + eps_norm)
        normed = (features * scale * gain_row).astype(jnp.bfloat16)
        query_weight = blend_small(mixing[1], src_query).astype(jnp.bfloat16)
        key_weight = blend_small(mixing[2], src_key).astype(jnp.bfloat16)
        value_weight = blend_small(mixing[3], src_value).astype(jnp.bfloat16)
        queries = jnp.dot(normed, query_weight, preferred_element_type=jnp.float32) + blend_small(mixing[1], src_qbias)
        key_rows = jnp.dot(normed, key_weight, preferred_element_type=jnp.float32) + blend_small(mixing[2], src_kbias)
        value_rows = (jnp.dot(normed, value_weight, preferred_element_type=jnp.float32) + blend_small(mixing[3], src_vbias)).astype(jnp.bfloat16)
        queries = rotate(queries.reshape(TOK, QH, DH), cosine_table[:, None, :], sine_table[:, None, :])
        queries = queries.reshape(TOK, KVH, per_group, DH)
        key_rows = rotate(key_rows.reshape(TOK, KVH, DH), cosine_table[:, None, :], sine_table[:, None, :])
        value_rows = value_rows.reshape(TOK, KVH, DH)
        shares = attention_shares(queries, key_rows, document_mask(length_row, TOK))
        result = jnp.einsum('gqts,sgd->tgqd', shares.astype(jnp.float32), value_rows.astype(jnp.float32))
        return result.reshape(TOK, QH * DH).astype(jnp.bfloat16)
    return lax.map(candidate, (layer_input, coef_index, lengths))
```

```python
import jax
import jax.numpy as jnp
from jax import lax
from jax.experimental import pallas as pl
from jax.experimental.pallas import tpu as pltpu
from jax.sharding import Mesh, PartitionSpec as P

QH = 32
KVH = 8
DH = 128
TOK = 256
PER = QH // KVH
CHUNKS = ((4, 5, 0), (1, 2, 3))
MIX_ROW = (1, 1, 1, 1, 2, 3)
WIRE = jnp.float16
TWIN = (0, 2, 1, 3)

eps_norm = 1e-06
rope_base = 1000000.0

VMEM = pl.BlockSpec(memory_space=pltpu.VMEM)
SMEM = pl.BlockSpec(memory_space=pltpu.SMEM)
LIMIT = 48 * 1024 * 1024


def pack_kernel(q_ref, k_ref, v_ref, *outs):
    for core in range(2):
        for x in range(4):
            group = x * 2 + core
            for chunk, out in zip(CHUNKS, outs):
                for at, block in enumerate(chunk):
                    if block < PER:
                        src, col = q_ref, (group * PER + block) * DH
                    else:
                        src, col = (k_ref if block == PER else v_ref), group * DH
                    out[core * 4 + x, :, :, at * DH : (at + 1) * DH] = src[:, :, col : col + DH]


def pack(src_query, src_key, src_value):
    rows = src_query.shape[1]
    return pl.pallas_call(
        pack_kernel,
        out_shape=[
            jax.ShapeDtypeStruct((8, 3, rows, len(chunk) * DH), jnp.bfloat16) for chunk in CHUNKS
        ],
        in_specs=[VMEM] * 3,
        out_specs=[VMEM] * len(CHUNKS),
        compiler_params=pltpu.CompilerParams(vmem_limit_bytes=LIMIT),
    )(src_query, src_key, src_value)


def column_runs(chunk):
    runs = []
    for at, block in enumerate(chunk):
        row = MIX_ROW[block]
        if runs and runs[-1][0] == row:
            runs[-1][2] = at + 1
        else:
            runs.append([row, at, at + 1])
    return runs


def product_kernel(chunk, where_ref, blend_ref, *rest):
    acts, pieces, out_ref, weights = rest[:8], rest[8:12], rest[12], rest[13]
    width = len(chunk) * DH
    for at, piece in enumerate(pieces):
        y = where_ref[at]
        for core in range(2):
            for pair in range(2):
                block = core * 4 + pair * 2
                for row, first, last in column_runs(chunk):
                    mixed = jnp.dot(
                        blend_ref[row - 1],
                        piece[block : block + 2, :, :, first * DH : last * DH].reshape(
                            192, (last - first) * DH
                        ),
                        preferred_element_type=jnp.float32,
                    ).astype(jnp.bfloat16)
                    for cand in range(8):
                        weights[cand, core, y, pair * 64 : pair * 64 + 64, first * DH : last * DH] = (
                            mixed[cand * 64 : cand * 64 + 64]
                        )
    own = where_ref[4]
    for piece in range(4):
        for hi in range(2):
            cand = piece * 2 + hi
            total = jnp.dot(
                acts[piece][hi],
                weights[cand, own].reshape(512, width),
                preferred_element_type=jnp.float32,
            )
            out_ref[where_ref[5 + cand]] = total + jnp.dot(
                acts[4 + TWIN[piece]][hi],
                weights[cand, 1 - own].reshape(512, width),
                preferred_element_type=jnp.float32,
            )


def product(chunk, where, blend, acts, pieces):
    width = len(chunk) * DH
    return pl.pallas_call(
        lambda *refs: product_kernel(chunk, *refs),
        out_shape=jax.ShapeDtypeStruct((8, TOK, width), jnp.float32),
        in_specs=[SMEM] + [VMEM] * 13,
        out_specs=VMEM,
        scratch_shapes=[pltpu.VMEM((8, 2, 4, 128, width), jnp.bfloat16)],
        compiler_params=pltpu.CompilerParams(vmem_limit_bytes=LIMIT),
        cost_estimate=pl.CostEstimate(
            flops=4 * 8 * TOK * 1024 * width, bytes_accessed=12 * 1024 * 1024, transcendentals=0
        ),
    )(where, blend, *acts, *pieces)


def blend_kernel(mix_ref, out_ref):
    row = lax.broadcasted_iota(jnp.int32, (64, 192), 0)
    col = lax.broadcasted_iota(jnp.int32, (64, 192), 1)
    upper = (col >= 96).astype(jnp.int32)
    same = ((row >> 5) == upper) & ((row & 31) == (col & 31))
    source = (col - 96 * upper) >> 5
    picks = [(same & (source == s)).astype(jnp.float32) for s in range(3)]
    for part in range(3):
        for cand in range(8):
            block = sum(mix_ref[cand, (part + 1) * 3 + s] * picks[s] for s in range(3))
            out_ref[part, cand * 64 : cand * 64 + 64] = block.astype(jnp.bfloat16)


def blend_matrix(mix):
    return pl.pallas_call(
        blend_kernel,
        out_shape=jax.ShapeDtypeStruct((3, 512, 192), jnp.bfloat16),
        in_specs=[SMEM],
        out_specs=VMEM,
    )(mix)


def attend_kernel(lengths_ref, cos_ref, sin_ref, bias_ref, *rest):
    totals, out_ref = rest[:-1], rest[-1]
    cosine, sine = cos_ref[...], sin_ref[...]

    def part(block):
        for chunk, total in zip(CHUNKS, totals):
            if block in chunk:
                at = chunk.index(block)
                return (
                    total[:, at * DH : (at + 1) * DH]
                    + bias_ref[:, block * DH : (block + 1) * DH]
                )

    def rotate(matrix):
        leading, trailing = matrix[:, : DH // 2], matrix[:, DH // 2 :]
        return jnp.concatenate(
            [leading * cosine - trailing * sine, trailing * cosine + leading * sine], axis=1
        )

    token = lax.broadcasted_iota(jnp.int32, (TOK, TOK), 0)
    other = lax.broadcasted_iota(jnp.int32, (TOK, TOK), 1)
    first = jnp.zeros((TOK, TOK), jnp.int32)
    end = jnp.int32(0)
    for doc in range(8):
        end = end + lengths_ref[0, doc]
        first = jnp.where(token >= end, end, first)
    allowed = (other >= first) & (other <= token)
    keys = rotate(part(PER))
    values = part(PER + 1).astype(jnp.bfloat16)
    for head in range(PER):
        scores = lax.dot_general(
            rotate(part(head)),
            keys,
            (((1,), (1,)), ((), ())),
            precision=lax.Precision.HIGHEST,
            preferred_element_type=jnp.float32,
        )
        scores = jnp.where(allowed, scores * DH ** (-0.5), -1e30)
        powers = jnp.exp(scores - jnp.max(scores, axis=-1, keepdims=True))
        shares = (powers / jnp.sum(powers, axis=-1, keepdims=True)).astype(jnp.bfloat16)
        out_ref[:, head * DH : (head + 1) * DH] = jnp.dot(
            shares, values, preferred_element_type=jnp.float32
        ).astype(jnp.bfloat16)


def attend(lengths, cosine, sine, bias, totals):
    return pl.pallas_call(
        attend_kernel,
        out_shape=jax.ShapeDtypeStruct((TOK, PER * DH), jnp.bfloat16),
        in_specs=[SMEM] + [VMEM] * (3 + len(totals)),
        out_specs=VMEM,
        compiler_params=pltpu.CompilerParams(vmem_limit_bytes=LIMIT),
    )(lengths, cosine, sine, bias, *totals)


def after(value, *others):
    return lax.optimization_barrier((value,) + others)[0]


def blend_small(mixing, source):
    source = source.astype(jnp.float32)
    return mixing[0] * source[0] + mixing[1] * source[1] + mixing[2] * source[2]


def rope_tables():
    positions = jnp.arange(TOK).astype(jnp.float32)
    exponent = jnp.arange(0, DH, 2).astype(jnp.float32) / DH
    angle = positions[:, None] * (rope_base ** (-exponent))[None, :]
    return jnp.cos(angle), jnp.sin(angle)


def ring(size, sign):
    return [
        (at * 2 + c, (at + (sign if c == 0 else -sign)) % size * 2 + c)
        for at in range(size)
        for c in range(2)
    ]


def shards(
    layer_input,
    coef_index,
    lengths,
    src_gain,
    src_query,
    src_key,
    src_value,
    src_qbias,
    src_kbias,
    src_vbias,
):
    y, zh, x = lax.axis_index("y"), lax.axis_index("zh"), lax.axis_index("x")
    zl, core = lax.axis_index("zl"), lax.axis_index("c")
    z = zh * 4 + zl
    sign = 1 - 2 * core
    mixing = (coef_index.astype(jnp.float32) - 4.0) / 16.0

    slabs = pack(src_query, src_key, src_value)
    routed = [lax.all_to_all(slab, ("c", "x"), 0, 0, tiled=True) for slab in slabs]

    held = layer_input[0]
    halves = [
        jnp.concatenate([held[:, (2 * b + h) * 128 : (2 * b + h + 1) * 128] for b in range(4)], axis=1)
        for h in range(2)
    ]
    own_half = jnp.where(zh == 0, halves[0], halves[1])
    send_half = jnp.where(zh == 0, halves[1], halves[0])
    other_half = lax.ppermute(send_half, "zh", [(0, 1), (1, 0)])
    wide = held.astype(jnp.float32)
    squares = jnp.sum(wide * wide, axis=-1).reshape(1, 2, 128)
    squares = lax.all_to_all(
        jnp.broadcast_to(squares, (8, 2, 128)), ("zl", "c"), 0, 0, tiled=True
    )
    scale = lax.rsqrt(jnp.sum(squares, axis=0) / 8192.0 + eps_norm)
    other_scale = lax.ppermute(scale, "zh", [(0, 1), (1, 0)])

    part_gain = lax.dynamic_slice_in_dim(src_gain, (zl * 2 + core) * 1024, 1024, 1)
    part_gain = [
        jnp.concatenate(
            [part_gain[:, (2 * b + h) * 128 : (2 * b + h + 1) * 128] for b in range(4)], axis=1
        )
        for h in range(2)
    ]
    part_gain = jnp.where(zh == 0, part_gain[0], part_gain[1])

    def normalise(half, row, which):
        coefs = lax.dynamic_index_in_dim(mixing, y * 8 + which * 4 + x, 0, keepdims=False)[0]
        gain = blend_small(coefs, part_gain)
        return (half.astype(jnp.float32) * row.reshape(TOK, 1) * gain[None, :]).astype(jnp.bfloat16)

    pair = jnp.stack([normalise(own_half, scale, zh), normalise(other_half, other_scale, 1 - zh)])
    xa = lax.ppermute(pair, ("x", "c"), ring(4, 1))
    xb = lax.ppermute(pair, ("x", "c"), ring(4, -1))
    xf = lax.ppermute(xa, ("x", "c"), ring(4, 1))
    acts = [pair, xa, xb, xf]
    acts = acts + [lax.ppermute(piece, "c", [(0, 1), (1, 0)]) for piece in acts]

    offsets = (4, 3, 2, 1, -3, -2, -1, 0)
    xs = [x, (x + 4 - sign) % 4, (x + 4 + sign) % 4, (x + 2) % 4]
    dests = [((zh + hi) % 2) * 4 + at for at in xs for hi in range(2)]
    ranks = [(sign * (dest - z) + 8) % 8 for dest in dests]
    slot_of = jnp.array([offsets.index(r if r < 5 else r - 8) for r in range(8)], jnp.int32)
    slots = slot_of[jnp.stack(ranks)]
    where = jnp.concatenate(
        [jnp.stack([y, (y + 4 - sign) % 4, (y + 4 + sign) % 4, (y + 2) % 4, core]), slots]
    ).astype(jnp.int32)
    mine = lax.dynamic_slice_in_dim(mixing, y * 8, 8, 0).reshape(8, 12)
    blend = blend_matrix(mine[jnp.stack(dests)])

    own_mix = lax.dynamic_index_in_dim(mixing, y * 8 + z, 0, keepdims=False)
    group = x * 2 + core
    bias = jnp.concatenate(
        [
            blend_small(own_mix[1], lax.dynamic_slice_in_dim(src_qbias, group * 512, 512, 1)),
            blend_small(own_mix[2], lax.dynamic_slice_in_dim(src_kbias, group * 128, 128, 1)),
            blend_small(own_mix[3], lax.dynamic_slice_in_dim(src_vbias, group * 128, 128, 1)),
        ]
    )[None, :]
    turn = [(i * 4 + j, j * 4 + i) for i in range(4) for j in range(4)]
    own_lengths = lax.ppermute(lengths, ("x", "zl"), turn)
    cosine, sine = rope_tables()

    routed[0], blend, bias, cosine, sine, where = lax.optimization_barrier(
        (routed[0], blend, bias, cosine, sine, where)
    )

    gathered = []
    for near in routed:
        a = lax.ppermute(near, ("y", "c"), ring(4, 1))
        b = lax.ppermute(near, ("y", "c"), ring(4, -1))
        far = lax.ppermute(a, ("y", "c"), ring(4, 1))
        gathered.append((near, a, b, far))

    totals = []
    for chunk, pieces in zip(CHUNKS, gathered):
        part = product(chunk, where, blend, acts, pieces)
        first = lax.optimization_barrier((part[0], part[4]))
        a, b = first[0].astype(WIRE), first[1].astype(WIRE)
        for step in range(4):
            a = lax.ppermute(a, ("zh", "zl", "c"), ring(8, 1))
            if step < 3:
                a = (a.astype(jnp.float32) + part[1 + step]).astype(WIRE)
                b = lax.ppermute(b, ("zh", "zl", "c"), ring(8, -1))
                if step < 2:
                    b = (b.astype(jnp.float32) + part[5 + step]).astype(WIRE)
        totals.append(a.astype(jnp.float32) + b.astype(jnp.float32) + part[7])

    result = attend(own_lengths, cosine, sine, bias, totals)
    return lax.ppermute(result, ("x", "zl"), turn)[None]


def solution(mesh):
    fine = Mesh(mesh.devices.reshape(4, 2, 4, 4, 2), ("y", "zh", "x", "zl", "c"))
    cand, tp = ("y", "zh", "x"), ("zl", "c")
    placed = (
        P(cand, None, tp),
        P(),
        P(cand, None),
        P(),
        P(None, tp + cand, None),
        P(None, tp + cand, None),
        P(None, tp + cand, None),
        P(),
        P(),
        P(),
    )
    return jax.shard_map(
        shards, mesh=fine, in_specs=placed, out_specs=P(cand, None, tp), check_vma=False
    )
```

```python
import jax
import jax.numpy as jnp
from jax import lax
from jax.experimental import pallas as pl
from jax.experimental.pallas import tpu as pltpu
from jax.sharding import Mesh, PartitionSpec as P

QH = 32
KVH = 8
DH = 128
TOK = 256
PER = QH // KVH
CHUNKS = ((0, 1, 2, 3), (4, 5))
MIX_ROW = (1, 1, 1, 1, 2, 3)
TWIN = (0, 2, 1, 3)
WIRE = jnp.float16

eps_norm = 1e-06
rope_base = 1000000.0

VMEM = pl.BlockSpec(memory_space=pltpu.VMEM)
SMEM = pl.BlockSpec(memory_space=pltpu.SMEM)
MIB = 1024 * 1024


def coef(coef_ref, cand, part, source):
    return (coef_ref[cand, part * 3 + source].astype(jnp.float32) - 4.0) * 0.0625


def front_kernel(where_ref, x_ref, q_ref, k_ref, v_ref, slab_ref, own_ref, send_ref, squares_ref):
    for core in range(2):
        for x in range(4):
            group, to = x * 2 + core, core * 4 + x
            wide = PER * DH
            slab_ref[to, :, :, :wide] = q_ref[:, :, group * wide : group * wide + wide]
            slab_ref[to, :, :, wide : wide + DH] = k_ref[:, :, group * DH : group * DH + DH]
            slab_ref[to, :, :, wide + DH :] = v_ref[:, :, group * DH : group * DH + DH]
    low = where_ref[0] == 0
    total = jnp.zeros((TOK, 128), jnp.float32)
    for block in range(4):
        even = x_ref[0, :, block * 256 : block * 256 + 128]
        odd = x_ref[0, :, block * 256 + 128 : block * 256 + 256]
        own_ref[:, block * 128 : block * 128 + 128] = jnp.where(low, even, odd)
        send_ref[:, block * 128 : block * 128 + 128] = jnp.where(low, odd, even)
        even, odd = even.astype(jnp.float32), odd.astype(jnp.float32)
        total = total + even * even + odd * odd
    squares_ref[...] = jnp.broadcast_to(
        jnp.sum(total.T, axis=0, keepdims=True), squares_ref.shape
    )


def front(where, layer_input, src_query, src_key, src_value):
    rows = src_query.shape[1]
    half = jax.ShapeDtypeStruct((TOK, 512), jnp.bfloat16)
    return pl.pallas_call(
        front_kernel,
        out_shape=[
            jax.ShapeDtypeStruct((8, 3, rows, (PER + 2) * DH), jnp.bfloat16),
            half,
            half,
            jax.ShapeDtypeStruct((8, TOK), jnp.float32),
        ],
        in_specs=[SMEM] + [VMEM] * 4,
        out_specs=[VMEM] * 4,
        compiler_params=pltpu.CompilerParams(vmem_limit_bytes=16 * MIB),
    )(where, layer_input, src_query, src_key, src_value)


def normalise_kernel(where_ref, coef_ref, own_ref, other_ref, squares_ref, gain_ref, out_ref):
    for hi, half in enumerate((own_ref, other_ref)):
        scale = lax.rsqrt(squares_ref[hi * 4 : hi * 4 + 1, :] * (1.0 / 8192.0) + eps_norm)
        scale = jnp.broadcast_to(scale, (128, TOK)).T
        cand = where_ref[2 + hi]
        weights = [coef(coef_ref, cand, 0, s) for s in range(3)]
        for block in range(4):
            start = pl.multiple_of(where_ref[1] + block * 256, 128)
            rows = [gain_ref[s : s + 1, pl.ds(start, 128)].astype(jnp.float32) for s in range(3)]
            gain = weights[0] * rows[0] + weights[1] * rows[1] + weights[2] * rows[2]
            lanes = slice(block * 128, block * 128 + 128)
            out_ref[hi, :, lanes] = (
                half[:, lanes].astype(jnp.float32) * scale * gain
            ).astype(jnp.bfloat16)


def normalise(where, coefs, own, other, squares, src_gain):
    return pl.pallas_call(
        normalise_kernel,
        out_shape=jax.ShapeDtypeStruct((2, TOK, 512), jnp.bfloat16),
        in_specs=[SMEM] * 2 + [VMEM] * 4,
        out_specs=VMEM,
        compiler_params=pltpu.CompilerParams(vmem_limit_bytes=8 * MIB),
    )(where, coefs, own, other, squares, src_gain)


def blend_kernel(cand_ref, coef_ref, out_ref):
    row = lax.broadcasted_iota(jnp.int32, (64, 192), 0)
    col = lax.broadcasted_iota(jnp.int32, (64, 192), 1)
    upper = (col >= 96).astype(jnp.int32)
    same = ((row >> 5) == upper) & ((row & 31) == (col & 31))
    source = (col - 96 * upper) >> 5
    picks = [(same & (source == s)).astype(jnp.float32) for s in range(3)]
    for part in range(3):
        for cand in range(8):
            block = sum(coef(coef_ref, cand_ref[cand], part + 1, s) * picks[s] for s in range(3))
            out_ref[part, cand * 64 : cand * 64 + 64] = block.astype(jnp.bfloat16)


def blend_matrix(cands, coefs):
    return pl.pallas_call(
        blend_kernel,
        out_shape=jax.ShapeDtypeStruct((3, 512, 192), jnp.bfloat16),
        in_specs=[SMEM] * 2,
        out_specs=VMEM,
        compiler_params=pltpu.CompilerParams(vmem_limit_bytes=8 * MIB),
    )(cands, coefs)


def column_runs(chunk):
    runs = []
    for at, block in enumerate(chunk):
        row = MIX_ROW[block]
        if runs and runs[-1][0] == row:
            runs[-1][2] = at + 1
        else:
            runs.append([row, at, at + 1])
    return runs


def product_kernel(chunk, where_ref, blend_ref, *rest):
    acts, pieces, out_ref, weights = rest[:8], rest[8:12], rest[12], rest[13]
    width = len(chunk) * DH
    for at, piece in enumerate(pieces):
        y = where_ref[at]
        for core in range(2):
            for pair in range(2):
                block = core * 4 + pair * 2
                for row, first, last in column_runs(chunk):
                    mixed = jnp.dot(
                        blend_ref[row - 1],
                        piece[block : block + 2, :, :, first * DH : last * DH].reshape(
                            192, (last - first) * DH
                        ),
                        preferred_element_type=jnp.float32,
                    ).astype(jnp.bfloat16)
                    for cand in range(8):
                        weights[cand, core, y, pair * 64 : pair * 64 + 64, first * DH : last * DH] = (
                            mixed[cand * 64 : cand * 64 + 64]
                        )
    own = where_ref[4]
    for piece in range(4):
        for hi in range(2):
            cand = piece * 2 + hi
            total = jnp.dot(
                acts[piece][hi],
                weights[cand, own].reshape(512, width),
                preferred_element_type=jnp.float32,
            )
            out_ref[where_ref[5 + cand]] = total + jnp.dot(
                acts[4 + TWIN[piece]][hi],
                weights[cand, 1 - own].reshape(512, width),
                preferred_element_type=jnp.float32,
            )


def product(chunk, where, blend, acts, pieces):
    width = len(chunk) * DH
    return pl.pallas_call(
        lambda *refs: product_kernel(chunk, *refs),
        out_shape=jax.ShapeDtypeStruct((8, TOK, width), jnp.float32),
        in_specs=[SMEM] + [VMEM] * 13,
        out_specs=VMEM,
        scratch_shapes=[pltpu.VMEM((8, 2, 4, 128, width), jnp.bfloat16)],
        compiler_params=pltpu.CompilerParams(vmem_limit_bytes=24 * MIB),
        cost_estimate=pl.CostEstimate(
            flops=4 * 8 * TOK * 1024 * width, bytes_accessed=12 * MIB, transcendentals=0
        ),
    )(where, blend, *acts, *pieces)


def attend_kernel(where_ref, coef_ref, lengths_ref, cos_ref, sin_ref, *rest):
    bias_refs, totals, out_ref = rest[:3], rest[3:-1], rest[-1]
    cosine, sine = cos_ref[...], sin_ref[...]
    cand, group = where_ref[0], where_ref[1]

    def part(block):
        for chunk, total in zip(CHUNKS, totals):
            if block in chunk:
                at = chunk.index(block)
                found = total[:, at * DH : (at + 1) * DH]
        row = MIX_ROW[block]
        column = group * (PER * DH) + block * DH if block < PER else group * DH
        lanes = pl.ds(pl.multiple_of(column, DH), DH)
        bias = bias_refs[row - 1]
        rows = [
            coef(coef_ref, cand, row, s) * bias[s : s + 1, lanes].astype(jnp.float32)
            for s in range(3)
        ]
        return found + (rows[0] + rows[1] + rows[2])

    def rotate(matrix):
        leading, trailing = matrix[:, : DH // 2], matrix[:, DH // 2 :]
        return jnp.concatenate(
            [leading * cosine - trailing * sine, trailing * cosine + leading * sine], axis=1
        )

    token = lax.broadcasted_iota(jnp.int32, (TOK, TOK), 0)
    other = lax.broadcasted_iota(jnp.int32, (TOK, TOK), 1)
    first = jnp.zeros((TOK, TOK), jnp.int32)
    end = jnp.int32(0)
    for doc in range(8):
        end = end + lengths_ref[0, doc]
        first = jnp.where(token >= end, end, first)
    allowed = (other >= first) & (other <= token)
    keys = rotate(part(PER))
    values = part(PER + 1).astype(jnp.bfloat16)
    for head in range(PER):
        scores = lax.dot_general(
            rotate(part(head)),
            keys,
            (((1,), (1,)), ((), ())),
            precision=lax.Precision.HIGHEST,
            preferred_element_type=jnp.float32,
        )
        scores = jnp.where(allowed, scores * DH ** (-0.5), -1e30)
        powers = jnp.exp(scores - jnp.max(scores, axis=-1, keepdims=True))
        shares = (powers / jnp.sum(powers, axis=-1, keepdims=True)).astype(jnp.bfloat16)
        out_ref[:, head * DH : (head + 1) * DH] = jnp.dot(
            shares, values, preferred_element_type=jnp.float32
        ).astype(jnp.bfloat16)


def attend(where, coefs, lengths, cosine, sine, biases, totals):
    return pl.pallas_call(
        attend_kernel,
        out_shape=jax.ShapeDtypeStruct((TOK, PER * DH), jnp.bfloat16),
        in_specs=[SMEM] * 3 + [VMEM] * (5 + len(totals)),
        out_specs=VMEM,
        compiler_params=pltpu.CompilerParams(vmem_limit_bytes=16 * MIB),
    )(where, coefs, lengths, cosine, sine, *biases, *totals)


def after(value, *others):
    return lax.optimization_barrier((value,) + others)[0]


def flip(value):
    return (value & 1) * 2 + (value >> 1)


def rope_tables():
    positions = jnp.arange(TOK).astype(jnp.float32)
    exponent = jnp.arange(0, DH, 2).astype(jnp.float32) / DH
    angle = positions[:, None] * (rope_base ** (-exponent))[None, :]
    return jnp.cos(angle), jnp.sin(angle)


def ring(size, sign):
    return [
        (at * 2 + c, (at + (sign if c == 0 else -sign)) % size * 2 + c)
        for at in range(size)
        for c in range(2)
    ]


def shards(
    layer_input,
    coef_index,
    lengths,
    src_gain,
    src_query,
    src_key,
    src_value,
    src_qbias,
    src_kbias,
    src_vbias,
):
    y, zh, x = lax.axis_index("y"), lax.axis_index("zh"), lax.axis_index("x")
    zl, core = lax.axis_index("zl"), lax.axis_index("c")
    z = zh * 4 + zl
    sign = 1 - 2 * core
    coefs = coef_index.reshape(32, 12)
    swap = [(0, 1), (1, 0)]

    def numbers(*values):
        return jnp.stack([jnp.asarray(v, jnp.int32) for v in values])

    slab, own_half, send_half, squares = front(
        numbers(zh), layer_input, src_query, src_key, src_value
    )

    slab = lax.all_to_all(slab, ("c", "x"), 0, 0, tiled=True)
    routed = [
        slab[:, :, :, chunk[0] * DH : (chunk[-1] + 1) * DH] for chunk in CHUNKS
    ]

    offsets = (4, 3, 2, 1, -3, -2, -1, 0)
    xs = [x, (x + 4 - sign) % 4, (x + 4 + sign) % 4, (x + 2) % 4]
    spots = [((zh + hi) % 2, at) for at in xs for hi in range(2)]
    slots = []
    for h, at in spots:
        rank = (sign * (h * 4 + flip(at ^ x) - z) + 8) % 8
        slots.append(sum(jnp.where(rank == o % 8, i, 0) for i, o in enumerate(offsets)))
    where = numbers(y, (y + 4 - sign) % 4, (y + 4 + sign) % 4, (y + 2) % 4, core, *slots)
    cands = numbers(*[y * 8 + h * 4 + at for h, at in spots])
    blend = blend_matrix(cands, coefs)
    cosine, sine = rope_tables()

    squares = after(squares, blend, cosine, sine, where)
    cross = [(i, i ^ 3) for i in range(4)]
    mine = squares + lax.ppermute(squares, "c", swap)
    theirs = lax.ppermute(squares, "zh", swap) + lax.ppermute(squares, ("zh", "c"), cross)
    squares = jnp.concatenate([mine[:4], theirs[:4]])
    other_half = lax.ppermute(send_half, "zh", swap)
    squares = squares + sum(
        lax.ppermute(squares, "zl", [(i, (i + d) % 4) for i in range(4)]) for d in (1, 2, 3)
    )

    gathered = []
    for near in routed:
        if gathered:
            near = after(near, *gathered[-1][1:3])
        a = lax.ppermute(near, ("y", "c"), ring(4, 1))
        b = lax.ppermute(near, ("y", "c"), ring(4, -1))
        if gathered:
            gathered.append((near, a, b))
        else:
            far = lax.ppermute(after(a, b), ("y", "c"), ring(4, 1))
            gathered.append((near, a, b, far))

    own = numbers(zh, (zl * 2 + core) * 1024 + zh * 128, y * 8 + zh * 4 + x, y * 8 + (1 - zh) * 4 + x)
    pair = normalise(own, coefs, own_half, other_half, after(squares, routed[0]), src_gain)
    xa = lax.ppermute(pair, ("x", "c"), ring(4, 1))
    xb = lax.ppermute(pair, ("x", "c"), ring(4, -1))
    xf = lax.ppermute(after(xa, xb), ("x", "c"), ring(4, 1))
    acts = [pair, xa, xb, xf]
    acts = acts + [lax.ppermute(piece, "c", swap) for piece in acts]

    taken = x ^ flip(zl)
    turn = [(i * 4 + j, (i ^ flip(j)) * 4 + i) for i in range(4) for j in range(4)]
    own_lengths = lax.ppermute(lengths, ("x", "zl"), [(t, s) for s, t in turn])

    totals = []
    for chunk, pieces in zip(CHUNKS, gathered):
        if totals:
            near, a, b = pieces
            far = lax.ppermute(after(a, b), ("y", "c"), ring(4, 1))
            pieces = (near, a, b, far)
        else:
            where = after(where, *gathered[1][1:])
        part = product(chunk, where, blend, acts, pieces)
        first = lax.optimization_barrier((part[0], part[4]))
        a, b = first[0].astype(WIRE), first[1].astype(WIRE)
        for step in range(4):
            a = lax.ppermute(a, ("zh", "zl", "c"), ring(8, 1))
            if step < 3:
                a = (a.astype(jnp.float32) + part[1 + step]).astype(WIRE)
                b = lax.ppermute(b, ("zh", "zl", "c"), ring(8, -1))
                if step < 2:
                    b = (b.astype(jnp.float32) + part[5 + step]).astype(WIRE)
        totals.append(a.astype(jnp.float32) + b.astype(jnp.float32) + part[7])

    where = numbers(y * 8 + zh * 4 + taken, x * 2 + core)
    biases = (src_qbias, src_kbias, src_vbias)
    result = attend(where, coefs, own_lengths, cosine, sine, biases, totals)
    return lax.ppermute(result, ("x", "zl"), turn)[None]


def solution(mesh):
    fine = Mesh(mesh.devices.reshape(4, 2, 4, 4, 2), ("y", "zh", "x", "zl", "c"))
    cand, tp = ("y", "zh", "x"), ("zl", "c")
    placed = (
        P(cand, None, tp),
        P(),
        P(cand, None),
        P(),
        P(None, tp + cand, None),
        P(None, tp + cand, None),
        P(None, tp + cand, None),
        P(),
        P(),
        P(),
    )
    return jax.shard_map(
        shards, mesh=fine, in_specs=placed, out_specs=P(cand, None, tp), check_vma=False
    )
```

```python
import jax
import jax.numpy as jnp
from jax import lax
from jax.experimental import pallas as pl
from jax.experimental.pallas import tpu as pltpu
from jax.sharding import Mesh, PartitionSpec as P

QH = 32
KVH = 8
DH = 128
TOK = 256
PER = QH // KVH
CHUNKS = ((0, 1, 2, 3), (4, 5))
MIX_ROW = (1, 1, 1, 1, 2, 3)
TWIN = (0, 2, 1, 3)
WIRE = jnp.float16

eps_norm = 1e-06
rope_base = 1000000.0

VMEM = pl.BlockSpec(memory_space=pltpu.VMEM)
SMEM = pl.BlockSpec(memory_space=pltpu.SMEM)
MIB = 1024 * 1024


def coef(coef_ref, cand, part, source):
    return (coef_ref[cand, part * 3 + source].astype(jnp.float32) - 4.0) * 0.0625


def front_kernel(where_ref, x_ref, q_ref, k_ref, v_ref, slab_ref, own_ref, send_ref, squares_ref):
    for core in range(2):
        for x in range(4):
            group, to = x * 2 + core, core * 4 + x
            wide = PER * DH
            slab_ref[to, :, :, :wide] = q_ref[:, :, group * wide : group * wide + wide]
            slab_ref[to, :, :, wide : wide + DH] = k_ref[:, :, group * DH : group * DH + DH]
            slab_ref[to, :, :, wide + DH :] = v_ref[:, :, group * DH : group * DH + DH]
    low = where_ref[0] == 0
    total = jnp.zeros((TOK, 128), jnp.float32)
    for block in range(4):
        even = x_ref[0, :, block * 256 : block * 256 + 128]
        odd = x_ref[0, :, block * 256 + 128 : block * 256 + 256]
        own_ref[:, block * 128 : block * 128 + 128] = jnp.where(low, even, odd)
        send_ref[:, block * 128 : block * 128 + 128] = jnp.where(low, odd, even)
        even, odd = even.astype(jnp.float32), odd.astype(jnp.float32)
        total = total + even * even + odd * odd
    squares_ref[...] = jnp.broadcast_to(
        jnp.sum(total.T, axis=0, keepdims=True), squares_ref.shape
    )


def front(where, layer_input, src_query, src_key, src_value):
    rows = src_query.shape[1]
    half = jax.ShapeDtypeStruct((TOK, 512), jnp.bfloat16)
    return pl.pallas_call(
        front_kernel,
        out_shape=[
            jax.ShapeDtypeStruct((8, 3, rows, (PER + 2) * DH), jnp.bfloat16),
            half,
            half,
            jax.ShapeDtypeStruct((8, TOK), jnp.float32),
        ],
        in_specs=[SMEM] + [VMEM] * 4,
        out_specs=[VMEM] * 4,
        compiler_params=pltpu.CompilerParams(vmem_limit_bytes=16 * MIB),
    )(where, layer_input, src_query, src_key, src_value)


def normalise_kernel(where_ref, coef_ref, own_ref, other_ref, squares_ref, gain_ref, out_ref):
    for hi, half in enumerate((own_ref, other_ref)):
        scale = lax.rsqrt(squares_ref[hi * 4 : hi * 4 + 1, :] * (1.0 / 8192.0) + eps_norm)
        scale = jnp.broadcast_to(scale, (128, TOK)).T
        cand = where_ref[2 + hi]
        weights = [coef(coef_ref, cand, 0, s) for s in range(3)]
        for block in range(4):
            start = pl.multiple_of(where_ref[1] + block * 256, 128)
            rows = [gain_ref[s : s + 1, pl.ds(start, 128)].astype(jnp.float32) for s in range(3)]
            gain = weights[0] * rows[0] + weights[1] * rows[1] + weights[2] * rows[2]
            lanes = slice(block * 128, block * 128 + 128)
            out_ref[hi, :, lanes] = (
                half[:, lanes].astype(jnp.float32) * scale * gain
            ).astype(jnp.bfloat16)


def normalise(where, coefs, own, other, squares, src_gain):
    return pl.pallas_call(
        normalise_kernel,
        out_shape=jax.ShapeDtypeStruct((2, TOK, 512), jnp.bfloat16),
        in_specs=[SMEM] * 2 + [VMEM] * 4,
        out_specs=VMEM,
        compiler_params=pltpu.CompilerParams(vmem_limit_bytes=8 * MIB),
    )(where, coefs, own, other, squares, src_gain)


def blend_kernel(cand_ref, coef_ref, out_ref):
    row = lax.broadcasted_iota(jnp.int32, (64, 192), 0)
    col = lax.broadcasted_iota(jnp.int32, (64, 192), 1)
    upper = (col >= 96).astype(jnp.int32)
    same = ((row >> 5) == upper) & ((row & 31) == (col & 31))
    source = (col - 96 * upper) >> 5
    picks = [(same & (source == s)).astype(jnp.float32) for s in range(3)]
    for part in range(3):
        for cand in range(8):
            block = sum(coef(coef_ref, cand_ref[cand], part + 1, s) * picks[s] for s in range(3))
            out_ref[part, cand * 64 : cand * 64 + 64] = block.astype(jnp.bfloat16)


def blend_matrix(cands, coefs):
    return pl.pallas_call(
        blend_kernel,
        out_shape=jax.ShapeDtypeStruct((3, 512, 192), jnp.bfloat16),
        in_specs=[SMEM] * 2,
        out_specs=VMEM,
        compiler_params=pltpu.CompilerParams(vmem_limit_bytes=8 * MIB),
    )(cands, coefs)


def column_runs(chunk):
    runs = []
    for at, block in enumerate(chunk):
        row = MIX_ROW[block]
        if runs and runs[-1][0] == row:
            runs[-1][2] = at + 1
        else:
            runs.append([row, at, at + 1])
    return runs


def product_kernel(chunk, where_ref, blend_ref, *rest):
    acts, pieces, out_ref, weights = rest[:8], rest[8:12], rest[12], rest[13]
    width = len(chunk) * DH
    for at, piece in enumerate(pieces):
        y = where_ref[at]
        for core in range(2):
            for pair in range(2):
                block = core * 4 + pair * 2
                for row, first, last in column_runs(chunk):
                    mixed = jnp.dot(
                        blend_ref[row - 1],
                        piece[block : block + 2, :, :, first * DH : last * DH].reshape(
                            192, (last - first) * DH
                        ),
                        preferred_element_type=jnp.float32,
                    ).astype(jnp.bfloat16)
                    for cand in range(8):
                        weights[cand, core, y, pair * 64 : pair * 64 + 64, first * DH : last * DH] = (
                            mixed[cand * 64 : cand * 64 + 64]
                        )
    own = where_ref[4]
    for piece in range(4):
        for hi in range(2):
            cand = piece * 2 + hi
            total = jnp.dot(
                acts[piece][hi],
                weights[cand, own].reshape(512, width),
                preferred_element_type=jnp.float32,
            )
            out_ref[where_ref[5 + cand]] = total + jnp.dot(
                acts[4 + TWIN[piece]][hi],
                weights[cand, 1 - own].reshape(512, width),
                preferred_element_type=jnp.float32,
            )


def product(chunk, where, blend, acts, pieces):
    width = len(chunk) * DH
    return pl.pallas_call(
        lambda *refs: product_kernel(chunk, *refs),
        out_shape=jax.ShapeDtypeStruct((8, TOK, width), jnp.float32),
        in_specs=[SMEM] + [VMEM] * 13,
        out_specs=VMEM,
        scratch_shapes=[pltpu.VMEM((8, 2, 4, 128, width), jnp.bfloat16)],
        compiler_params=pltpu.CompilerParams(vmem_limit_bytes=24 * MIB),
        cost_estimate=pl.CostEstimate(
            flops=4 * 8 * TOK * 1024 * width, bytes_accessed=12 * MIB, transcendentals=0
        ),
    )(where, blend, *acts, *pieces)


def attend_kernel(where_ref, coef_ref, lengths_ref, cos_ref, sin_ref, *rest):
    bias_refs, totals, out_ref = rest[:3], rest[3:-1], rest[-1]
    cosine, sine = cos_ref[...], sin_ref[...]
    cand, group = where_ref[0], where_ref[1]

    def part(block):
        for chunk, total in zip(CHUNKS, totals):
            if block in chunk:
                at = chunk.index(block)
                found = total[:, at * DH : (at + 1) * DH]
        row = MIX_ROW[block]
        column = group * (PER * DH) + block * DH if block < PER else group * DH
        lanes = pl.ds(pl.multiple_of(column, DH), DH)
        bias = bias_refs[row - 1]
        rows = [
            coef(coef_ref, cand, row, s) * bias[s : s + 1, lanes].astype(jnp.float32)
            for s in range(3)
        ]
        return found + (rows[0] + rows[1] + rows[2])

    def rotate(matrix):
        leading, trailing = matrix[:, : DH // 2], matrix[:, DH // 2 :]
        return jnp.concatenate(
            [leading * cosine - trailing * sine, trailing * cosine + leading * sine], axis=1
        )

    token = lax.broadcasted_iota(jnp.int32, (TOK, TOK), 0)
    other = lax.broadcasted_iota(jnp.int32, (TOK, TOK), 1)
    first = jnp.zeros((TOK, TOK), jnp.int32)
    end = jnp.int32(0)
    for doc in range(8):
        end = end + lengths_ref[0, doc]
        first = jnp.where(token >= end, end, first)
    allowed = (other >= first) & (other <= token)
    keys = rotate(part(PER))
    values = part(PER + 1).astype(jnp.bfloat16)
    for head in range(PER):
        scores = lax.dot_general(
            rotate(part(head)),
            keys,
            (((1,), (1,)), ((), ())),
            precision=lax.Precision.HIGHEST,
            preferred_element_type=jnp.float32,
        )
        scores = jnp.where(allowed, scores * DH ** (-0.5), -1e30)
        powers = jnp.exp(scores - jnp.max(scores, axis=-1, keepdims=True))
        shares = (powers / jnp.sum(powers, axis=-1, keepdims=True)).astype(jnp.bfloat16)
        out_ref[:, head * DH : (head + 1) * DH] = jnp.dot(
            shares, values, preferred_element_type=jnp.float32
        ).astype(jnp.bfloat16)


def attend(where, coefs, lengths, cosine, sine, biases, totals):
    return pl.pallas_call(
        attend_kernel,
        out_shape=jax.ShapeDtypeStruct((TOK, PER * DH), jnp.bfloat16),
        in_specs=[SMEM] * 3 + [VMEM] * (5 + len(totals)),
        out_specs=VMEM,
        compiler_params=pltpu.CompilerParams(vmem_limit_bytes=16 * MIB),
    )(where, coefs, lengths, cosine, sine, *biases, *totals)


def after(value, *others):
    return lax.optimization_barrier((value,) + others)[0]


def flip(value):
    return (value & 1) * 2 + (value >> 1)


def rope_tables():
    positions = jnp.arange(TOK).astype(jnp.float32)
    exponent = jnp.arange(0, DH, 2).astype(jnp.float32) / DH
    angle = positions[:, None] * (rope_base ** (-exponent))[None, :]
    return jnp.cos(angle), jnp.sin(angle)


def ring(size, sign):
    return [
        (at * 2 + c, (at + (sign if c == 0 else -sign)) % size * 2 + c)
        for at in range(size)
        for c in range(2)
    ]


def shards(
    layer_input,
    coef_index,
    lengths,
    src_gain,
    src_query,
    src_key,
    src_value,
    src_qbias,
    src_kbias,
    src_vbias,
):
    y, zh, x = lax.axis_index("y"), lax.axis_index("zh"), lax.axis_index("x")
    zl, core = lax.axis_index("zl"), lax.axis_index("c")
    z = zh * 4 + zl
    sign = 1 - 2 * core
    coefs = coef_index.reshape(32, 12)
    swap = [(0, 1), (1, 0)]

    def numbers(*values):
        return jnp.stack([jnp.asarray(v, jnp.int32) for v in values])

    slab, own_half, send_half, squares = front(
        numbers(zh), layer_input, src_query, src_key, src_value
    )

    slab = lax.all_to_all(slab, ("c", "x"), 0, 0, tiled=True)
    routed = [
        slab[:, :, :, chunk[0] * DH : (chunk[-1] + 1) * DH] for chunk in CHUNKS
    ]

    offsets = (4, 3, 2, 1, -3, -2, -1, 0)
    xs = [x, (x + 4 - sign) % 4, (x + 4 + sign) % 4, (x + 2) % 4]
    spots = [((zh + hi) % 2, at) for at in xs for hi in range(2)]
    slots = []
    for h, at in spots:
        rank = (sign * (h * 4 + flip(at ^ x) - z) + 8) % 8
        slots.append(sum(jnp.where(rank == o % 8, i, 0) for i, o in enumerate(offsets)))
    where = numbers(y, (y + 4 - sign) % 4, (y + 4 + sign) % 4, (y + 2) % 4, core, *slots)
    cands = numbers(*[y * 8 + h * 4 + at for h, at in spots])
    blend = blend_matrix(cands, coefs)
    cosine, sine = rope_tables()

    squares = after(squares, blend, cosine, sine, where)
    cross = [(i, i ^ 3) for i in range(4)]
    mine = squares + lax.ppermute(squares, "c", swap)
    theirs = lax.ppermute(squares, "zh", swap) + lax.ppermute(squares, ("zh", "c"), cross)
    squares = jnp.concatenate([mine[:4], theirs[:4]])
    other_half = lax.ppermute(send_half, "zh", swap)
    squares = squares + sum(
        lax.ppermute(squares, "zl", [(i, (i + d) % 4) for i in range(4)]) for d in (1, 2, 3)
    )

    taken = x ^ flip(zl)
    turn = [(i * 4 + j, (i ^ flip(j)) * 4 + i) for i in range(4) for j in range(4)]
    gathered = []
    for near in routed:
        if gathered:
            near = after(near, *gathered[-1][1:3])
        a = lax.ppermute(near, ("y", "c"), ring(4, 1))
        b = lax.ppermute(near, ("y", "c"), ring(4, -1))
        if gathered:
            gathered.append((near, a, b))
        else:
            far = lax.ppermute(after(a, b), ("y", "c"), ring(4, 1))
            gathered.append((near, a, b, far))

    own = numbers(zh, (zl * 2 + core) * 1024 + zh * 128, y * 8 + zh * 4 + x, y * 8 + (1 - zh) * 4 + x)
    pair = normalise(own, coefs, own_half, other_half, after(squares, routed[0]), src_gain)
    xa = lax.ppermute(pair, ("x", "c"), ring(4, 1))
    xb = lax.ppermute(pair, ("x", "c"), ring(4, -1))
    own_lengths = lax.ppermute(after(lengths, pair), ("x", "zl"), [(t, s) for s, t in turn])
    xf = lax.ppermute(after(xa, xb, own_lengths), ("x", "c"), ring(4, 1))
    acts = [pair, xa, xb, xf]
    acts = acts + [lax.ppermute(piece, "c", swap) for piece in acts]

    totals = []
    for chunk, pieces in zip(CHUNKS, gathered):
        if totals:
            near, a, b = pieces
            far = lax.ppermute(after(a, b), ("y", "c"), ring(4, 1))
            pieces = (near, a, b, far)
            where = after(where, part)
        else:
            where = after(where, *gathered[1][1:])
        part = product(chunk, where, blend, acts, pieces)
        first = lax.optimization_barrier((part[0], part[4]))
        a, b = first[0].astype(WIRE), first[1].astype(WIRE)
        for step in range(4):
            a = lax.ppermute(a, ("zh", "zl", "c"), ring(8, 1))
            if step < 3:
                a = (a.astype(jnp.float32) + part[1 + step]).astype(WIRE)
                b = lax.ppermute(b, ("zh", "zl", "c"), ring(8, -1))
                if step < 2:
                    b = (b.astype(jnp.float32) + part[5 + step]).astype(WIRE)
        totals.append(a.astype(jnp.float32) + b.astype(jnp.float32) + part[7])

    where = numbers(y * 8 + zh * 4 + taken, x * 2 + core)
    biases = (src_qbias, src_kbias, src_vbias)
    result = attend(where, coefs, own_lengths, cosine, sine, biases, totals)
    return lax.ppermute(result, ("x", "zl"), turn)[None]


def solution(mesh):
    fine = Mesh(mesh.devices.reshape(4, 2, 4, 4, 2), ("y", "zh", "x", "zl", "c"))
    cand, tp = ("y", "zh", "x"), ("zl", "c")
    placed = (
        P(cand, None, tp),
        P(),
        P(cand, None),
        P(),
        P(None, tp + cand, None),
        P(None, tp + cand, None),
        P(None, tp + cand, None),
        P(),
        P(),
        P(),
    )
    return jax.shard_map(
        shards, mesh=fine, in_specs=placed, out_specs=P(cand, None, tp), check_vma=False
    )
```
